256 devices in a mesh: island: 4 (over z_hi), fsdp: 64 (over y, z_lo, x, core).
Axes of the slice: x: 4, y: 4, z: 8 (z_hi: 4, z_lo: 2; z = z_hi * 2 + z_lo), core: 2. Of those that a mesh axis runs over, the one named last changes fastest.
Arguments:
- params: float32 [18432, 7168], P(('island', 'fsdp')), as said below
- momentum: float32 [18432, 7168], P(('island', 'fsdp')), as said below
- payload: bfloat16 [18432, 7168], P(('island', 'fsdp')), may hold values from -1 to 1, as said below
- scales: float32 [18432, 56], P(('island', 'fsdp')), may hold values from 0 to 1, as said below
- bounds: int32 [4, 65], replicated, may hold values from 0 to 3072, as said below
Outputs:
- params_out: float32 [18432, 7168], P(('island', 'fsdp'))
- momentum_out: float32 [18432, 7168], P(('island', 'fsdp'))
- mean_payload: bfloat16 [18432, 7168], P(('island', 'fsdp'))
- mean_scales: float32 [18432, 56], P(('island', 'fsdp'))
The draws below stay inside these ranges and needn't reach their ends.
Inputs may be any that keep to these rules, and one draw needn't show every extreme that they name: `bounds`: row i lists the first global row of each of island i's shards and then the end; entry j lies within 12 of j * 48, entry 0 is 0 and the last is 3072; every island has a shard of exactly 72 rows. `payload`: slots outside a device's shard hold zeros. `scales`: slots outside a device's shard hold zeros. `params`: every island holds the same global rows; slots outside a device's shard hold zeros. `momentum`: every island holds the same global rows; slots outside a device's shard hold zeros.
All inputs are finite; a program needn't handle non-finite values. Where the reference program divides by a largest or mean magnitude, that divisor is 1e-20 or more.
Results may differ from the reference program's by a relative error of at most 0.017.
Values may be sent and summed in bfloat16 or wider, within the bound.
No kernel may reach another device: no remote copies, remote signals or barrier semaphores. Data moves between devices by JAX's collectives and lax.ppermute only.
A program may use at most 64 MiB of HBM per device.

```python
import jax
import jax.numpy as jnp

D = 7168
QB = 128
NB = 56
ROWS_DEV = 48
HALF = 12
CAP = 72
ROWS = 3072
N_ISLAND = 4
N_FSDP = 64


def layout_starts(key):
    key = jax.random.fold_in(key, 11)
    offsets = jax.random.randint(key, (N_ISLAND, N_FSDP + 1), -HALF, HALF + 1)
    chosen = jax.random.randint(jax.random.fold_in(key, 1), (N_ISLAND, 1), 1, N_FSDP - 1)
    column = jnp.arange(N_FSDP + 1, dtype=jnp.int32)[None, :]
    offsets = jnp.where(column == chosen, -HALF, offsets)
    offsets = jnp.where(column == chosen + 1, HALF, offsets)
    offsets = jnp.where((column == 0) | (column == N_FSDP), 0, offsets)
    return (column * ROWS_DEV + offsets).astype(jnp.int32)


def live_layout(starts):
    shard_index = jnp.arange(N_FSDP, dtype=jnp.int32)
    global_row = shard_index[:, None] * ROWS_DEV - HALF + jnp.arange(CAP, dtype=jnp.int32)[None, :]
    inside = (global_row[None] >= starts[:, :-1, None]) & (global_row[None] < starts[:, 1:, None])
    return (global_row, inside.astype(jnp.float32))


def lay_out(values, starts):
    global_row, inside = live_layout(starts)
    picked = values[jnp.clip(global_row, 0, ROWS - 1)]
    return (picked[None] * inside[..., None]).reshape(N_ISLAND * N_FSDP * CAP, values.shape[1])


def draw_bounds(key, part):
    return layout_starts(key)


def draw_params(key, part):
    starts = layout_starts(key)
    key = jax.random.fold_in(key, 3)
    values = jax.random.normal(key, (ROWS, D), jnp.float32)
    return lay_out(values, starts).astype(jnp.float32)


def draw_momentum(key, part):
    starts = layout_starts(key)
    key = jax.random.fold_in(key, 5)
    values = 0.5 * jax.random.normal(key, (ROWS, D), jnp.float32)
    return lay_out(values, starts).astype(jnp.float32)


def draw_payload(key, part):
    starts = layout_starts(key)
    key = jax.random.fold_in(key, 7)
    shape = (N_ISLAND, N_FSDP, CAP, D)
    values = jax.random.uniform(key, shape, jnp.float32, -1.0, 1.0)
    global_row, inside = live_layout(starts)
    return (values * inside[..., None]).reshape(N_ISLAND * N_FSDP * CAP, D).astype(jnp.bfloat16)


def draw_scales(key, part):
    starts = layout_starts(key)
    key = jax.random.fold_in(key, 9)
    shape = (N_ISLAND, N_FSDP, CAP, NB)
    values = jnp.exp(jax.random.uniform(key, shape, jnp.float32, jnp.log(0.05), 0.0))
    global_row, inside = live_layout(starts)
    return (values * inside[..., None]).reshape(N_ISLAND * N_FSDP * CAP, NB).astype(jnp.float32)


def setup_inputs(seed: int = 0) -> dict:
    keys = jax.random.split(jax.random.key(seed), 6)
    params = draw_params(jax.random.fold_in(keys[5], 71), 0)
    momentum = draw_momentum(jax.random.fold_in(keys[5], 71), 0)
    payload = draw_payload(jax.random.fold_in(keys[5], 71), 0)
    scales = draw_scales(jax.random.fold_in(keys[5], 71), 0)
    bounds = draw_bounds(jax.random.fold_in(keys[5], 71), 0)
    return dict(params=params, momentum=momentum, payload=payload, scales=scales, bounds=bounds)


momentum_keep = 0.9
outer_rate = 0.7
block_eps = 1e-6


def live_masks(bounds):
    shard_index = jnp.arange(N_FSDP, dtype=jnp.int32)
    global_row = shard_index[:, None] * ROWS_DEV - HALF + jnp.arange(CAP, dtype=jnp.int32)[None, :]
    starts = bounds[:, :-1][:, :, None]
    stops = bounds[:, 1:][:, :, None]
    inside = (global_row[None] >= starts) & (global_row[None] < stops)
    return inside.astype(jnp.float32)


def dequantize(coded, block_scale):
    shape = coded.shape
    blocks = coded.astype(jnp.float32).reshape(shape[:-1] + (NB, QB))
    return (blocks * block_scale[..., None]).reshape(shape)


def requantize(summed):
    shape = summed.shape
    blocks = summed.reshape(shape[:-1] + (NB, QB))
    block_scale = jnp.max(jnp.abs(blocks), axis=-1) + block_eps
    coded = (blocks / block_scale[..., None]).astype(jnp.bfloat16).reshape(shape)
    return coded, block_scale


def fold_core(extended):
    centre = extended[:, HALF:HALF + ROWS_DEV]
    from_left = jnp.concatenate([jnp.zeros_like(extended[:1, CAP - HALF:]), extended[:-1, CAP - HALF:]], axis=0)
    from_right = jnp.concatenate([extended[1:, :HALF], jnp.zeros_like(extended[:1, :HALF])], axis=0)
    spare = ROWS_DEV - HALF
    return centre + jnp.pad(from_left, ((0, 0), (0, spare), (0, 0))) + jnp.pad(from_right, ((0, 0), (spare, 0), (0, 0)))


def spread_core(core):
    left_rim = jnp.concatenate([jnp.zeros_like(core[:1, ROWS_DEV - HALF:]), core[:-1, ROWS_DEV - HALF:]], axis=0)
    right_rim = jnp.concatenate([core[1:, :HALF], jnp.zeros_like(core[:1, :HALF])], axis=0)
    return jnp.concatenate([left_rim, core, right_rim], axis=1)


def reference(params, momentum, payload, scales, bounds):
    layout = (N_ISLAND, N_FSDP, CAP)
    masks = live_masks(bounds)
    codes_all = payload.reshape(layout + (D,))
    scales_all = scales.reshape(layout + (NB,))
    summed = jnp.zeros((N_FSDP, ROWS_DEV, D), jnp.float32)
    for island_pos in range(N_ISLAND):
        terms = dequantize(codes_all[island_pos], scales_all[island_pos]) * masks[island_pos][:, :, None]
        summed = summed + fold_core(terms)
    coded, block_scale = requantize(summed)
    coded_ext = spread_core(coded)
    scale_ext = spread_core(block_scale)
    mask_col = masks[..., None]
    mean_payload = coded_ext[None] * mask_col.astype(jnp.bfloat16)
    mean_scales = scale_ext[None] * mask_col
    delta = (dequantize(coded_ext, scale_ext) / N_ISLAND)[None] * mask_col
    momentum_now = momentum.reshape(layout + (D,))
    params_now = params.reshape(layout + (D,))
    momentum_out = momentum_keep * momentum_now + delta
    params_out = params_now - outer_rate * (delta + momentum_keep * momentum_out)
    total_rows = N_ISLAND * N_FSDP * CAP
    return (params_out.reshape(total_rows, D), momentum_out.reshape(total_rows, D),
            mean_payload.reshape(total_rows, D), mean_scales.reshape(total_rows, NB))
```

```python
import functools

import jax
import jax.numpy as jnp
from jax import lax
from jax.experimental import pallas as pl
from jax.experimental.pallas import tpu as pltpu
from jax.sharding import PartitionSpec as P

ROWS_DEV = 48
HALF = 12
BAND = 24
QB = 128

momentum_keep = 0.9
outer_rate = 0.7
block_eps = 1e-06

F32 = jnp.float32
BF16 = jnp.bfloat16
AXES = ("island", "fsdp")
PAIRINGS = ({0: 1, 1: 0, 2: 3, 3: 2}, {0: 3, 3: 0, 1: 2, 2: 1})


def island_swap(value, step):
    shards = lax.axis_size("fsdp")
    pairs = [
        (i * shards + j, PAIRINGS[(j + step) % 2][i] * shards + j)
        for i in range(4)
        for j in range(shards)
    ]
    return lax.ppermute(value, AXES, pairs)


def inner_swap(value):
    return lax.ppermute(value, "fsdp", [(j, j ^ 1) for j in range(lax.axis_size("fsdp"))])


def outer_swap(value):
    count = lax.axis_size("fsdp")
    pairs = [(j, (j + 1) % count if j & 1 else (j - 1) % count) for j in range(count)]
    return lax.ppermute(value, "fsdp", pairs)


def local_call(body, out_shapes, info, *arrays, cost=1 << 20, **kwargs):
    vmem = pl.BlockSpec(memory_space=pltpu.VMEM)
    return pl.pallas_call(
        body,
        out_shape=out_shapes,
        in_specs=[pl.BlockSpec(memory_space=pltpu.SMEM)] + [vmem] * len(arrays),
        out_specs=jax.tree.map(lambda _: vmem, out_shapes),
        cost_estimate=pl.CostEstimate(flops=cost, bytes_accessed=cost, transcendentals=0),
        **kwargs,
    )(info, *arrays)


def live_rows(info_ref, first, rows, width):
    row = lax.broadcasted_iota(jnp.int32, (rows, width), 0) + first
    return ((row >= info_ref[0]) & (row < info_ref[1])).astype(F32)


def terms_body(info, payload, scales, mid_send, mid_keep, in_send, in_keep, out_send, out_keep):
    half = payload.shape[1] // 2
    blocks = half // QB

    def fill(band, part, target):
        rows = slice(band * BAND, (band + 1) * BAND)
        live_scales = scales[rows, :] * live_rows(info, band * BAND, BAND, scales.shape[1])
        for k in range(blocks):
            g = part * blocks + k
            scale = live_scales[:, g : g + 1]
            block = payload[rows, g * QB : (g + 1) * QB].astype(F32) * scale
            target[:, k * QB : (k + 1) * QB] = block.astype(target.dtype)

    for a in range(2):

        @pl.when(info[2] == a)
        def _(a=a):
            fill(1, 1 - a, mid_send)
            fill(1, a, mid_keep)

    for c in range(2):

        @pl.when(info[4] == c)
        def _(c=c):
            inner, outer = (2, 0) if c == 0 else (0, 2)
            fill(outer, c, out_send)
            fill(outer, 1 - c, out_keep)
            fill(inner, 1 - c, in_send)
            fill(inner, c, in_keep)


def fold_body(info, mid_send, mid_keep, in_keep, in_recv, send, keep):
    wide, narrow = mid_send.shape[1], in_keep.shape[1] // 2
    send[:, :wide] = mid_send[...]
    keep[:, :wide] = mid_keep[...]
    for a in range(2):

        @pl.when(info[2] == a)
        def _(a=a):
            for part, target in ((1 - a, send), (a, keep)):
                cols = slice(part * narrow, (part + 1) * narrow)
                total = in_keep[:, cols] + in_recv[:, cols].astype(F32)
                target[:, wide:] = total.astype(target.dtype)


def fold_outer_body(info, out_keep, out_recv, send, keep):
    width = out_keep.shape[1] // 2
    for a in range(2):

        @pl.when(info[2] == a)
        def _(a=a):
            for part, target in ((1 - a, send), (a, keep)):
                cols = slice(part * width, (part + 1) * width)
                total = out_keep[:, cols] + out_recv[:, cols].astype(F32)
                target[...] = total.astype(target.dtype)


def split_body(pieces, info, keep, recv, send, keep_next):
    for b in range(2):

        @pl.when(info[3] == b)
        def _(b=b):
            at = 0
            for width in pieces:
                half = width // 2
                for part, target in ((1 - b, send), (b, keep_next)):
                    cols = slice(at + part * half, at + (part + 1) * half)
                    total = keep[:, cols] + recv[:, cols].astype(F32)
                    target[:, at // 2 : at // 2 + half] = total.astype(target.dtype)
                at += width


def join_body(pieces, which, info, own, recv, out):
    for b in range(2):

        @pl.when(info[which] == b)
        def _(b=b):
            at = 0
            for width in pieces:
                half = width // 2
                src = slice(at // 2, at // 2 + half)
                for part, source in ((b, own), (1 - b, recv)):
                    out[:, at + part * half : at + (part + 1) * half] = source[:, src]
                at += width


def reduce_band(info, send, keep, pieces):
    rows, width = send.shape
    recv = island_swap(send, 0)
    send, keep = local_call(
        functools.partial(split_body, pieces),
        [
            jax.ShapeDtypeStruct((rows, width // 2), BF16),
            jax.ShapeDtypeStruct((rows, width // 2), F32),
        ],
        info,
        keep,
        recv,
    )
    recv = island_swap(send, 1)
    quarter = (keep + recv.astype(F32)).astype(BF16)
    other = island_swap(quarter, 1)
    return local_call(
        functools.partial(join_body, pieces, 3),
        jax.ShapeDtypeStruct((rows, width), BF16),
        info,
        quarter,
        other,
    )


def step_body(info, own1, recv1, in_mine, in_other, out_mine, out_other, params, momentum,
              params_out, momentum_out, payload_out, scales_out):
    width = params.shape[1]
    half = width // 2
    blocks = half // QB
    a, c = info[2], info[4]
    lane = lax.broadcasted_iota(jnp.int32, (BAND, QB), 1)

    def band(first, source):
        rows = pl.ds(first, BAND)
        live = live_rows(info, first, BAND, QB)
        scale_row = jnp.zeros((BAND, QB), F32)
        for g in range(2 * blocks):
            cols = slice(g * QB, (g + 1) * QB)
            summed = source(g // blocks, slice((g % blocks) * QB, (g % blocks + 1) * QB)).astype(F32)
            block_scale = jnp.max(jnp.abs(summed), axis=1, keepdims=True) + block_eps
            coded = (summed * (1.0 / block_scale)).astype(BF16).astype(F32) * live
            block_live = block_scale * live
            delta = coded * (block_live * 0.25)
            moved = momentum_keep * momentum[rows, cols] + delta
            momentum_out[rows, cols] = moved
            params_out[rows, cols] = params[rows, cols] - outer_rate * (
                delta + momentum_keep * moved
            )
            payload_out[rows, cols] = coded.astype(BF16)
            scale_row = jnp.where(lane == g, block_live, scale_row)
        scales_out[rows, :] = scale_row[:, : 2 * blocks]

    def pick(flag, one, two):
        return lambda part, cols: jnp.where(flag == part, one[:, cols], two[:, cols])

    inner_first = pl.multiple_of((1 - c) * (2 * BAND), 16)
    outer_first = pl.multiple_of(c * (2 * BAND), 16)
    band(BAND, pick(a, own1, recv1))
    band(inner_first, pick(c, in_mine, in_other))
    band(outer_first, pick(1 - c, out_mine, out_other))


def shards(params, momentum, payload, scales, bounds):
    slots, width = payload.shape
    half = width // 2
    island_pos = lax.axis_index("island")
    shard_pos = lax.axis_index("fsdp")
    origin = shard_pos * ROWS_DEV - HALF
    odd = shard_pos & 1
    low, high = island_pos & 1, island_pos >> 1
    bit_a = jnp.where(odd == 0, low ^ high, high)
    bit_b = jnp.where(odd == 0, high, low ^ high)
    info = jnp.stack(
        [
            bounds[island_pos, shard_pos] - origin,
            bounds[island_pos, shard_pos + 1] - origin,
            bit_a,
            bit_b,
            odd,
        ]
    ).astype(jnp.int32)

    def shape(columns, dtype):
        return jax.ShapeDtypeStruct((BAND, columns), dtype)

    mid_send, mid_keep, in_send, in_keep, out_send, out_keep = local_call(
        terms_body, [shape(half, BF16), shape(half, F32)] * 3, info, payload, scales
    )
    out_recv = outer_swap(out_send)
    in_recv = inner_swap(in_send)
    wide = half + half // 2
    send1, keep1 = local_call(
        fold_body, [shape(wide, BF16), shape(wide, F32)], info, mid_send, mid_keep, in_keep, in_recv
    )
    own1 = reduce_band(info, send1, keep1, (half, half // 2))
    send2, keep2 = local_call(
        fold_outer_body, [shape(half // 2, BF16), shape(half // 2, F32)], info, out_keep, out_recv
    )
    own2 = reduce_band(info, send2, keep2, (half // 2,))
    recv2 = island_swap(own2, 0)
    recv1 = island_swap(own1, 0)
    join = functools.partial(join_body, (half,), 2)
    out_mine = local_call(join, shape(half, BF16), info, own2, recv2)
    out_other = outer_swap(out_mine)
    in_mine = local_call(join, shape(half, BF16), info, own1[:, half:], recv1[:, half:])
    in_other = inner_swap(in_mine)
    return local_call(
        step_body,
        [
            jax.ShapeDtypeStruct((slots, width), F32),
            jax.ShapeDtypeStruct((slots, width), F32),
            jax.ShapeDtypeStruct((slots, width), BF16),
            jax.ShapeDtypeStruct((slots, width // QB), F32),
        ],
        info,
        own1[:, :half],
        recv1[:, :half],
        in_mine,
        in_other,
        out_mine,
        out_other,
        params,
        momentum,
        compiler_params=pltpu.CompilerParams(vmem_limit_bytes=40 << 20),
    )


def solution(mesh):
    spec = P(("island", "fsdp"), None)
    return jax.shard_map(
        shards, mesh=mesh, in_specs=(spec,) * 4 + (P(),), out_specs=(spec,) * 4, check_vma=False
    )
```

```python
import jax
import jax.numpy as jnp
from jax import lax
from jax.experimental import pallas as pl
from jax.experimental.pallas import tpu as pltpu
from jax.sharding import PartitionSpec as P

ROWS_DEV = 48
HALF = 12
BAND = 24
QB = 128

momentum_keep = 0.9
outer_rate = 0.7
block_eps = 1e-06

F32 = jnp.float32
BF16 = jnp.bfloat16
AXES = ("island", "fsdp")
PAIRINGS = ({0: 1, 1: 0, 2: 3, 3: 2}, {0: 3, 3: 0, 1: 2, 2: 1})


def island_swap(value, step):
    shards = lax.axis_size("fsdp")
    pairs = [
        (i * shards + j, PAIRINGS[(j + step) % 2][i] * shards + j)
        for i in range(4)
        for j in range(shards)
    ]
    return lax.ppermute(value, AXES, pairs)


def inner_swap(value):
    return lax.ppermute(value, "fsdp", [(j, j ^ 1) for j in range(lax.axis_size("fsdp"))])


def outer_swap(value):
    count = lax.axis_size("fsdp")
    pairs = [(j, (j + 1) % count if j & 1 else (j - 1) % count) for j in range(count)]
    return lax.ppermute(value, "fsdp", pairs)


def place(bounds):
    island, shard = lax.axis_index("island"), lax.axis_index("fsdp")
    origin = shard * ROWS_DEV - HALF
    odd = shard & 1
    low, high = island & 1, island >> 1
    bit_a = jnp.where(odd == 0, low ^ high, high)
    bit_b = jnp.where(odd == 0, high, low ^ high)
    return bounds[island, shard] - origin, bounds[island, shard + 1] - origin, bit_a, bit_b, odd


def live_rows(span, first, rows, width):
    row = lax.broadcasted_iota(jnp.int32, (rows, width), 0) + first
    return ((row >= span[0]) & (row < span[1])).astype(F32)


def local_call(body, outs, bounds, *arrays, grant, scratch=()):
    vmem = pl.BlockSpec(memory_space=pltpu.VMEM)
    return pl.pallas_call(
        body,
        out_shape=[jax.ShapeDtypeStruct(s, d) for s, d in outs],
        in_specs=[pl.BlockSpec(memory_space=pltpu.SMEM)] + [vmem] * len(arrays),
        out_specs=[vmem] * len(outs),
        scratch_shapes=scratch,
        cost_estimate=pl.CostEstimate(flops=1 << 20, bytes_accessed=1 << 20, transcendentals=0),
        compiler_params=pltpu.CompilerParams(vmem_limit_bytes=grant << 20),
    )(bounds, *arrays)


def terms_body(bounds, payload, scales, mid_send, mid_keep, in_send, out_send, out_first, out_keep,
               rows_scales):
    lo, hi, a, b, c = place(bounds)
    blocks = payload.shape[1] // QB
    half, eighth = blocks // 2, blocks // 8
    slots = payload.shape[0]
    rows_scales[:, :] = jnp.zeros(rows_scales.shape, F32)
    rows_scales[:, :blocks] = jnp.transpose(scales[...]) * live_rows((lo, hi), 0, slots, blocks)

    def fill(first, start, count, target, at=0):
        rows = pl.ds(first, BAND)
        local = pltpu.roll(rows_scales[rows, :], lax.rem(QB - start, QB), 1)
        for k in range(count):
            cols = pl.ds(pl.multiple_of((start + k) * QB, QB), QB)
            block = payload[rows, cols].astype(F32) * local[:, k : k + 1]
            target[:, (at + k) * QB : (at + k + 1) * QB] = block.astype(target.dtype)

    inner = pl.multiple_of((1 - c) * (2 * BAND), 16)
    outer = pl.multiple_of(c * (2 * BAND), 16)
    for u in range(2):
        for v in range(2):
            mine = (a ^ 1 ^ u) * 2 + (b ^ 1 ^ v)
            theirs = (b ^ 1 ^ u) * 2 + (a ^ 1 ^ v)
            fill(outer, c * half + theirs * eighth, eighth, out_send.at[2 * u + v])
            fill(inner, (1 - c) * half + theirs * eighth, eighth, in_send.at[2 * u + v])
    for u in range(2):
        for v in range(2):
            mine = (a ^ 1 ^ u) * 2 + (b ^ 1 ^ v)
            wide = (mid_send, mid_keep)[u].at[v]
            fill(BAND, mine * 2 * eighth, 2 * eighth, wide)
            fill(inner, c * half + mine * eighth, eighth, wide, 2 * eighth)
            fill(outer, (1 - c) * half + mine * eighth, eighth, (out_first, out_keep)[u].at[v])


def add_to(total, part):
    return (total.astype(F32) + part.astype(F32)).astype(total.dtype)


def reduce_band(send, keep):
    recv = island_swap(send, 0)
    send = (keep[0] + recv[0].astype(F32)).astype(BF16)
    keep = keep[1] + recv[1].astype(F32)
    recv = island_swap(send, 1)
    quarter = (keep + recv.astype(F32)).astype(BF16)
    other = island_swap(quarter, 1)
    return jnp.stack([quarter, other])


def step_body(bounds, own1, recv1, in_other, own2, recv2, out_other, params, momentum,
              params_out, momentum_out, payload_out, scales_out, rows_scales):
    lo, hi, a, b, c = place(bounds)
    blocks = params.shape[1] // QB
    half, fourth, eighth = blocks // 2, blocks // 4, blocks // 8
    lane = lax.broadcasted_iota(jnp.int32, (BAND, QB), 1)

    def band(first, source):
        rows = pl.ds(first, BAND)
        live = live_rows((lo, hi), first, BAND, QB)
        scale_row = jnp.zeros((BAND, QB), F32)
        for g in range(blocks):
            cols = slice(g * QB, (g + 1) * QB)
            summed = source(g).astype(F32)
            block_scale = jnp.max(jnp.abs(summed), axis=1, keepdims=True) + block_eps
            coded = (summed * (1.0 / block_scale)).astype(BF16).astype(F32) * live
            block_live = block_scale * live
            delta = coded * (block_live * 0.25)
            moved = momentum_keep * momentum[rows, cols] + delta
            momentum_out[rows, cols] = moved
            params_out[rows, cols] = params[rows, cols] - outer_rate * (
                delta + momentum_keep * moved
            )
            payload_out[rows, cols] = coded.astype(BF16)
            scale_row = jnp.where(lane == g, block_live, scale_row)
        rows_scales[rows, :] = scale_row

    def mid(g):
        part, quarter, k = g // half, g // fourth % 2, g % fourth
        cols = slice(k * QB, (k + 1) * QB)
        return jnp.where(a == part, own1[quarter ^ b, :, cols], recv1[quarter ^ b, :, cols])

    def side(mine_half, own, recv, at, other):
        def source(g):
            part, quarter, k = g % half // fourth, g // eighth % 2, g % eighth
            near = slice((at + k) * QB, (at + k + 1) * QB)
            far = slice(k * QB, (k + 1) * QB)
            mine = jnp.where(a == part, own[quarter ^ b, :, near], recv[quarter ^ b, :, near])
            theirs = other[2 * (part ^ b) + (quarter ^ a), :, far]
            return jnp.where(mine_half == g // half, mine, theirs)

        return source

    band(BAND, mid)
    band(pl.multiple_of((1 - c) * (2 * BAND), 16), side(c, own1, recv1, fourth, in_other))
    band(pl.multiple_of(c * (2 * BAND), 16), side(1 - c, own2, recv2, 0, out_other))
    scales_out[...] = jnp.transpose(rows_scales[...])[:blocks, :]


def shards(params, momentum, payload, scales, bounds):
    slots, width = payload.shape
    fourth, eighth = width // 4, width // 8
    wide = fourth + eighth
    mid_send, mid_keep, in_send, out_send, out_first, out_keep = local_call(
        terms_body,
        [
            ((2, BAND, wide), BF16),
            ((2, BAND, wide), F32),
            ((4, BAND, eighth), BF16),
            ((4, BAND, eighth), BF16),
            ((2, BAND, eighth), BF16),
            ((2, BAND, eighth), F32),
        ],
        bounds,
        payload,
        scales.T,
        grant=8,
        scratch=[pltpu.VMEM((slots, QB), F32)],
    )
    out_recv = outer_swap(out_send)
    in_recv = inner_swap(in_send)
    send1 = mid_send.at[:, :, fourth:].set(add_to(mid_send[:, :, fourth:], in_recv[:2]))
    keep1 = mid_keep.at[:, :, fourth:].set(add_to(mid_keep[:, :, fourth:], in_recv[2:]))
    own1 = reduce_band(send1, keep1)
    own2 = reduce_band(add_to(out_first, out_recv[:2]), add_to(out_keep, out_recv[2:]))
    recv2 = island_swap(own2, 0)
    out_other = outer_swap(jnp.concatenate([own2, recv2]))
    recv1 = island_swap(own1, 0)
    in_other = inner_swap(jnp.concatenate([own1[:, :, fourth:], recv1[:, :, fourth:]]))
    params_out, momentum_out, payload_out, scales_out = local_call(
        step_body,
        [
            ((slots, width), F32),
            ((slots, width), F32),
            ((slots, width), BF16),
            ((width // QB, slots), F32),
        ],
        bounds,
        own1,
        recv1,
        in_other,
        own2,
        recv2,
        out_other,
        params,
        momentum,
        grant=20,
        scratch=[pltpu.VMEM((slots, QB), F32)],
    )
    return params_out, momentum_out, payload_out, scales_out.T


def solution(mesh):
    spec = P(("island", "fsdp"), None)
    return jax.shard_map(
        shards, mesh=mesh, in_specs=(spec,) * 4 + (P(),), out_specs=(spec,) * 4, check_vma=False
    )
```

```python
import jax
import jax.numpy as jnp
from jax import lax
from jax.experimental import pallas as pl
from jax.experimental.pallas import tpu as pltpu
from jax.sharding import PartitionSpec as P

ROWS_DEV = 48
HALF = 12
BAND = 24
QB = 128

momentum_keep = 0.9
outer_rate = 0.7
block_eps = 1e-06

F32 = jnp.float32
BF16 = jnp.bfloat16
AXES = ("island", "fsdp")
PAIRINGS = ({0: 1, 1: 0, 2: 3, 3: 2}, {0: 3, 3: 0, 1: 2, 2: 1})


def island_swap(value, step):
    shards = lax.axis_size("fsdp")
    pairs = [
        (i * shards + j, PAIRINGS[(j + step) % 2][i] * shards + j)
        for i in range(4)
        for j in range(shards)
    ]
    return lax.ppermute(value, AXES, pairs)


def inner_swap(value):
    return lax.ppermute(value, "fsdp", [(j, j ^ 1) for j in range(lax.axis_size("fsdp"))])


def outer_swap(value):
    count = lax.axis_size("fsdp")
    pairs = [(j, (j + 1) % count if j & 1 else (j - 1) % count) for j in range(count)]
    return lax.ppermute(value, "fsdp", pairs)


def place():
    island, odd = lax.axis_index("island"), lax.axis_index("fsdp") & 1
    low, high = island & 1, island >> 1
    return jnp.where(odd == 0, low ^ high, high), jnp.where(odd == 0, high, low ^ high), odd


VMEM = pl.BlockSpec(memory_space=pltpu.VMEM)
HBM = pl.BlockSpec(memory_space=pltpu.HBM)


def local_call(body, outs, ins, *arrays, grant=2, aliases=None, scratch=(), cost=1):
    return pl.pallas_call(
        body,
        out_shape=[jax.ShapeDtypeStruct(s, d) for s, d, _ in outs],
        in_specs=ins,
        out_specs=[space for _, _, space in outs],
        scratch_shapes=scratch,
        input_output_aliases=aliases or {},
        cost_estimate=pl.CostEstimate(
            flops=cost << 20, bytes_accessed=cost << 20, transcendentals=0
        ),
        compiler_params=pltpu.CompilerParams(vmem_limit_bytes=grant << 20),
    )(*arrays)


def fill(payload, rows_scales, first, start, count, target, at=0):
    rows = pl.ds(first, BAND)
    local = pltpu.roll(rows_scales[rows, :], lax.rem(QB - start, QB), 1)
    for k in range(count):
        cols = pl.ds(pl.multiple_of((start + k) * QB, QB), QB)
        block = payload[rows, cols].astype(F32) * local[:, k : k + 1]
        target[:, (at + k) * QB : (at + k + 1) * QB] = block.astype(target.dtype)


def side_rows(odd):
    return pl.multiple_of((1 - odd) * (2 * BAND), 16), pl.multiple_of(odd * (2 * BAND), 16)


def edge_terms_body(payload_in, scales_in, bounds_in, out_send, in_send, payload, rows_scales, live,
                    scales, bounds, sems):
    _, b, c = place()
    slots, width = payload.shape
    blocks = width // QB
    half, fourth = blocks // 2, blocks // 4
    copies = [pltpu.make_async_copy(bounds_in, bounds, sems.at[0])]
    copies.append(pltpu.make_async_copy(scales_in, scales, sems.at[1]))
    for n, part in enumerate((c, 1 - c)):
        cols = pl.ds(pl.multiple_of(part * (width // 2), QB), width // 2)
        copies.append(
            pltpu.make_async_copy(payload_in.at[:, cols], payload.at[:, cols], sems.at[2 + n])
        )
    for copy in copies:
        copy.start()
    copies[0].wait()
    island, shard = lax.axis_index("island"), lax.axis_index("fsdp")
    origin = shard * ROWS_DEV - HALF
    row = lax.broadcasted_iota(jnp.int32, (slots, QB), 0) + origin
    live[...] = ((row >= bounds[island, shard]) & (row < bounds[island, shard + 1])).astype(F32)
    rows_scales[...] = jnp.zeros(rows_scales.shape, F32)
    copies[1].wait()
    rows_scales[:, :blocks] = jnp.transpose(scales[...]) * live[:, :blocks]
    inner, outer = side_rows(c)
    for copy, first, start, target in (
        (copies[2], outer, c * half, out_send),
        (copies[3], inner, (1 - c) * half, in_send),
    ):
        copy.wait()
        for u in range(2):
            fill(payload, rows_scales, first, start + (b ^ 1 ^ u) * fourth, fourth, target.at[u])


def mid_terms_body(payload, rows_scales, send, keep):
    a = place()[0]
    half = payload.shape[1] // QB // 2
    fill(payload, rows_scales, BAND, (1 - a) * half, half, send)
    fill(payload, rows_scales, BAND, a * half, half, keep)


def side_terms_body(payload, rows_scales, in_first, in_keep, out_first, out_keep):
    a, _, c = place()
    blocks = payload.shape[1] // QB
    half, fourth = blocks // 2, blocks // 4
    inner, outer = side_rows(c)
    for part, near, far in ((1 - a, in_first, out_first), (a, in_keep, out_keep)):
        fill(payload, rows_scales, inner, c * half + part * fourth, fourth, near)
        fill(payload, rows_scales, outer, (1 - c) * half + part * fourth, fourth, far)


def add_to(total, part):
    return (total.astype(F32) + part.astype(F32)).astype(total.dtype)


def reduce_band(send, keep):
    total = add_to(island_swap(send, 0), keep)
    return add_to(total, island_swap(total, 1))


def step_band(first, source, live, params, momentum, params_out, momentum_out, coded_out,
              scale_out, params_new, momentum_new, sems):
    rows = pl.ds(first, BAND)
    blocks = params.shape[1] // QB
    fourth = blocks // 4
    lane = lax.broadcasted_iota(jnp.int32, (BAND, QB), 1)
    alive = live[rows, :]
    scale_row = jnp.zeros((BAND, QB), F32)
    copies = []
    for g in range(blocks):
        cols = slice(g * QB, (g + 1) * QB)
        summed = source(g).astype(F32)
        block_scale = jnp.max(jnp.abs(summed), axis=1, keepdims=True) + block_eps
        coded = (summed * (1.0 / block_scale)).astype(BF16).astype(F32) * alive
        block_live = block_scale * alive
        delta = coded * (block_live * 0.25)
        moved = momentum_keep * momentum[rows, cols] + delta
        momentum_new[:, cols] = moved
        params_new[:, cols] = params[rows, cols] - outer_rate * (delta + momentum_keep * moved)
        coded_out[:, cols] = coded.astype(BF16)
        scale_row = jnp.where(lane == g, block_live, scale_row)
        if g % fourth == fourth - 1:
            part = slice((g + 1 - fourth) * QB, (g + 1) * QB)
            for n, (new, out) in enumerate(
                ((params_new, params_out), (momentum_new, momentum_out))
            ):
                copy = pltpu.make_async_copy(
                    new.at[:, part], out.at[rows, part], sems.at[n, g // fourth]
                )
                copy.start()
                copies.append(copy)
    scale_out[...] = scale_row
    return copies


def side_source(blocks, mine_half, own, recv, other):
    a, b, _ = place()
    half, fourth = blocks // 2, blocks // 4

    def source(g):
        part, k = g % half // fourth, g % fourth
        cols = slice(k * QB, (k + 1) * QB)
        mine = jnp.where(a == part, own[:, cols], recv[:, cols])
        theirs = other[part ^ b, :, cols]
        return jnp.where(mine_half == g // half, mine, theirs)

    return source


def mid_step_body(own, recv, live, params, momentum, params_out, momentum_out, coded, scale,
                  *scratch):
    a = place()[0]
    blocks = params.shape[1] // QB
    half = blocks // 2

    def source(g):
        cols = slice(g % half * QB, (g % half + 1) * QB)
        return jnp.where(a == g // half, own[:, cols], recv[:, cols])

    for copy in step_band(BAND, source, live, params, momentum, params_out, momentum_out, coded,
                          scale, *scratch):
        copy.wait()


def inner_step_body(own, recv, other, live, params, momentum, _p, _m, params_out, momentum_out,
                    coded, scale, *scratch):
    c = place()[2]
    blocks = params.shape[1] // QB
    source = side_source(blocks, c, own, recv, other)
    for copy in step_band(side_rows(c)[0], source, live, params, momentum, params_out,
                          momentum_out, coded, scale, *scratch):
        copy.wait()


def outer_step_body(own, recv, other, coded_mid, scale_mid, coded_in, scale_in, live, params,
                    momentum, _p, _m, params_out, momentum_out, payload_out, scales_out, payload,
                    rows_scales, scales, *scratch):
    c = place()[2]
    blocks = params.shape[1] // QB
    inner, outer = side_rows(c)
    payload[pl.ds(BAND, BAND), :] = coded_mid[...]
    payload[pl.ds(inner, BAND), :] = coded_in[...]
    rows_scales[pl.ds(BAND, BAND), :] = scale_mid[...]
    rows_scales[pl.ds(inner, BAND), :] = scale_in[...]
    source = side_source(blocks, 1 - c, own, recv, other)
    copies = step_band(outer, source, live, params, momentum, params_out, momentum_out,
                       payload.at[pl.ds(outer, BAND)], rows_scales.at[pl.ds(outer, BAND)], *scratch)
    sems = scratch[-1]
    copies.append(pltpu.make_async_copy(payload, payload_out, sems.at[2, 0]))
    copies[-1].start()
    scales[...] = jnp.transpose(rows_scales[...])[:blocks, :]
    copies.append(pltpu.make_async_copy(scales, scales_out, sems.at[2, 1]))
    copies[-1].start()
    for copy in copies:
        copy.wait()


def shards(params, momentum, payload, scales, bounds):
    slots, width = payload.shape
    half, fourth, blocks = width // 2, width // 4, width // QB
    out_send, in_send, payload_near, rows_scales, live = local_call(
        edge_terms_body,
        [
            ((2, BAND, fourth), BF16, VMEM),
            ((2, BAND, fourth), BF16, VMEM),
            ((slots, width), BF16, VMEM),
            ((slots, QB), F32, VMEM),
            ((slots, QB), F32, VMEM),
        ],
        [HBM, HBM, HBM],
        *(pltpu.with_memory_space_constraint(x, pltpu.HBM) for x in (payload, scales.T, bounds)),
        scratch=[
            pltpu.VMEM((blocks, slots), F32),
            pltpu.SMEM(bounds.shape, jnp.int32),
            pltpu.SemaphoreType.DMA((4,)),
        ],
    )
    out_recv = outer_swap(out_send)
    in_recv = inner_swap(in_send)
    near = (payload_near, rows_scales)
    mid_send, mid_keep = local_call(
        mid_terms_body, [((BAND, half), BF16, VMEM), ((BAND, half), F32, VMEM)], [VMEM] * 2, *near
    )
    in_first, in_keep, out_first, out_keep = local_call(
        side_terms_body,
        [((BAND, fourth), BF16, VMEM), ((BAND, fourth), F32, VMEM)] * 2,
        [VMEM] * 2,
        *near,
    )
    own_mid = reduce_band(mid_send, mid_keep)
    own_in = reduce_band(add_to(in_first, in_recv[0]), add_to(in_keep, in_recv[1]))
    own_out = reduce_band(add_to(out_first, out_recv[0]), add_to(out_keep, out_recv[1]))
    recv_mid = island_swap(own_mid, 0)
    recv_out = island_swap(own_out, 0)
    recv_in = island_swap(own_in, 0)
    out_other = outer_swap(jnp.stack([own_out, recv_out]))
    in_other = inner_swap(jnp.stack([own_in, recv_in]))

    whole = ((slots, width), F32, HBM)
    band = [((BAND, width), BF16, VMEM), ((BAND, QB), F32, VMEM)]
    scratch = [
        pltpu.VMEM((BAND, width), F32),
        pltpu.VMEM((BAND, width), F32),
        pltpu.SemaphoreType.DMA((3, 4)),
    ]
    state = (live, params, momentum)
    params_out, momentum_out, coded_mid, scale_mid = local_call(
        mid_step_body, [whole, whole] + band, [VMEM] * 5, own_mid, recv_mid, *state,
        grant=4, scratch=scratch, cost=24,
    )
    params_out, momentum_out, coded_in, scale_in = local_call(
        inner_step_body, [whole, whole] + band, [VMEM] * 6 + [HBM] * 2, own_in, recv_in, in_other,
        *state, params_out, momentum_out,
        grant=4, scratch=scratch, cost=4, aliases={6: 0, 7: 1},
    )
    params_out, momentum_out, payload_out, scales_out = local_call(
        outer_step_body,
        [whole, whole, ((slots, width), BF16, HBM), ((blocks, slots), F32, HBM)],
        [VMEM] * 10 + [HBM] * 2,
        own_out, recv_out, out_other, coded_mid, scale_mid, coded_in, scale_in,
        *state, params_out, momentum_out,
        grant=6, cost=4, aliases={10: 0, 11: 1},
        scratch=[
            pltpu.VMEM((slots, width), BF16),
            pltpu.VMEM((slots, QB), F32),
            pltpu.VMEM((blocks, slots), F32),
        ] + scratch,
    )
    return params_out, momentum_out, payload_out, scales_out.T


def solution(mesh):
    spec = P(("island", "fsdp"), None)
    return jax.shard_map(
        shards, mesh=mesh, in_specs=(spec,) * 4 + (P(),), out_specs=(spec,) * 4, check_vma=False
    )
```

```python
import jax
import jax.numpy as jnp
from jax import lax
from jax.experimental import pallas as pl
from jax.experimental.pallas import tpu as pltpu
from jax.sharding import PartitionSpec as P

ROWS_DEV = 48
HALF = 12
BAND = 24
QB = 128

momentum_keep = 0.9
outer_rate = 0.7
block_eps = 1e-06

F32 = jnp.float32
BF16 = jnp.bfloat16
AXES = ("island", "fsdp")
PAIRINGS = ({0: 1, 1: 0, 2: 3, 3: 2}, {0: 3, 3: 0, 1: 2, 2: 1})


def island_swap(value, step):
    shards = lax.axis_size("fsdp")
    pairs = [
        (i * shards + j, PAIRINGS[(j + step) % 2][i] * shards + j)
        for i in range(4)
        for j in range(shards)
    ]
    return lax.ppermute(value, AXES, pairs)


def inner_swap(value):
    return lax.ppermute(value, "fsdp", [(j, j ^ 1) for j in range(lax.axis_size("fsdp"))])


def outer_swap(value):
    count = lax.axis_size("fsdp")
    pairs = []
    for i in range(4):
        for j in range(count):
            near = j + 1 if j & 1 else j - 1
            inside = 0 <= near < count
            pairs.append((i * count + j, i * count + near if inside else PAIRINGS[0][i] * count + j))
    return jnp.where(at_end(), value, lax.ppermute(value, AXES, pairs))


def place():
    island, odd = lax.axis_index("island"), lax.axis_index("fsdp") & 1
    low, high = island & 1, island >> 1
    return jnp.where(odd == 0, low ^ high, high), jnp.where(odd == 0, high, low ^ high), odd


VMEM = pl.BlockSpec(memory_space=pltpu.VMEM)
HBM = pl.BlockSpec(memory_space=pltpu.HBM)


def local_call(body, outs, ins, *arrays, grant=2, aliases=None, scratch=(), cost=1):
    return pl.pallas_call(
        body,
        out_shape=[jax.ShapeDtypeStruct(s, d) for s, d, _ in outs],
        in_specs=ins,
        out_specs=[space for _, _, space in outs],
        scratch_shapes=scratch,
        input_output_aliases=aliases or {},
        cost_estimate=pl.CostEstimate(
            flops=cost << 20, bytes_accessed=cost << 20, transcendentals=0
        ),
        compiler_params=pltpu.CompilerParams(vmem_limit_bytes=grant << 20),
    )(*arrays)


def at_end():
    shard = lax.axis_index("fsdp")
    return (shard == 0) | (shard == lax.axis_size("fsdp") - 1)


def turned(block):
    swapped = jnp.concatenate([block[HALF:], block[:HALF]])
    return jnp.where(at_end(), swapped, block)


def fill(payload, rows_scales, first, start, count, target, turn=lambda block: block):
    rows = pl.ds(first, BAND)
    local = pltpu.roll(rows_scales[rows, :], lax.rem(QB - start, QB), 1)
    for k in range(count):
        cols = pl.ds(pl.multiple_of((start + k) * QB, QB), QB)
        block = payload[rows, cols].astype(F32) * local[:, k : k + 1]
        target[:, k * QB : (k + 1) * QB] = turn(block).astype(target.dtype)


def side_rows(odd):
    return pl.multiple_of((1 - odd) * (2 * BAND), 16), pl.multiple_of(odd * (2 * BAND), 16)


def outer_terms_body(payload_in, scales_in, bounds_in, out_send, payload, rows_scales, live, scales,
                     bounds, sems):
    a, b, c = place()
    slots, width = payload.shape
    blocks = width // QB
    half, fourth = blocks // 2, blocks // 4
    copies = [pltpu.make_async_copy(bounds_in, bounds, sems.at[0])]
    copies.append(pltpu.make_async_copy(scales_in, scales, sems.at[1]))
    for n, part in enumerate((c, 1 - c)):
        cols = pl.ds(pl.multiple_of(part * (width // 2), QB), width // 2)
        copies.append(
            pltpu.make_async_copy(payload_in.at[:, cols], payload.at[:, cols], sems.at[2 + n])
        )
    for copy in copies:
        copy.start()
    copies[0].wait()
    island, shard = lax.axis_index("island"), lax.axis_index("fsdp")
    origin = shard * ROWS_DEV - HALF
    row = lax.broadcasted_iota(jnp.int32, (slots, QB), 0) + origin
    live[...] = ((row >= bounds[island, shard]) & (row < bounds[island, shard + 1])).astype(F32)
    rows_scales[...] = jnp.zeros(rows_scales.shape, F32)
    copies[1].wait()
    rows_scales[:, :blocks] = jnp.transpose(scales[...]) * live[:, :blocks]
    outer = side_rows(c)[1]
    copies[2].wait()
    for u in range(2):
        part = (jnp.where(at_end(), a, b) ^ 1 ^ u) * fourth
        fill(payload, rows_scales, outer, c * half + part, fourth, out_send.at[u], turned)
    copies[3].wait()


def mid_terms_body(payload, rows_scales, in_send, send, keep):
    a, b, c = place()
    blocks = payload.shape[1] // QB
    half, fourth = blocks // 2, blocks // 4
    for u in range(2):
        start = (1 - c) * half + (b ^ 1 ^ u) * fourth
        fill(payload, rows_scales, side_rows(c)[0], start, fourth, in_send.at[u])
    fill(payload, rows_scales, BAND, (1 - a) * half, half, send)
    fill(payload, rows_scales, BAND, a * half, half, keep)


def side_terms_body(payload, rows_scales, in_first, in_keep, out_first, out_keep):
    a, _, c = place()
    blocks = payload.shape[1] // QB
    half, fourth = blocks // 2, blocks // 4
    inner, outer = side_rows(c)
    for part, near, far in ((1 - a, in_first, out_first), (a, in_keep, out_keep)):
        fill(payload, rows_scales, inner, c * half + part * fourth, fourth, near)
        fill(payload, rows_scales, outer, (1 - c) * half + part * fourth, fourth, far)


def add_to(total, part):
    return (total.astype(F32) + part.astype(F32)).astype(total.dtype)


def after(value, *others):
    return lax.optimization_barrier((value, others))[0]


def step_band(first, source, live, params, momentum, params_out, momentum_out, coded_out,
              scale_out, params_new, momentum_new, sems):
    rows = pl.ds(first, BAND)
    blocks = params.shape[1] // QB
    fourth = blocks // 4
    lane = lax.broadcasted_iota(jnp.int32, (BAND, QB), 1)
    alive = live[rows, :]
    scale_row = jnp.zeros((BAND, QB), F32)
    copies = []
    for g in range(blocks):
        cols = slice(g * QB, (g + 1) * QB)
        summed = source(g)
        block_scale = jnp.max(jnp.abs(summed), axis=1, keepdims=True) + block_eps
        coded = (summed * (1.0 / block_scale)).astype(BF16).astype(F32) * alive
        block_live = block_scale * alive
        delta = coded * (block_live * 0.25)
        moved = momentum_keep * momentum[rows, cols] + delta
        momentum_new[:, cols] = moved
        params_new[:, cols] = params[rows, cols] - outer_rate * (delta + momentum_keep * moved)
        coded_out[:, cols] = coded.astype(BF16)
        scale_row = jnp.where(lane == g, block_live, scale_row)
        if g % fourth == fourth - 1:
            part = slice((g + 1 - fourth) * QB, (g + 1) * QB)
            for n, (new, out) in enumerate(
                ((params_new, params_out), (momentum_new, momentum_out))
            ):
                copy = pltpu.make_async_copy(
                    new.at[:, part], out.at[rows, part], sems.at[n, g // fourth]
                )
                copy.start()
                copies.append(copy)
    scale_out[...] = scale_row
    return copies


def side_source(blocks, mine_half, near_part, own, recv, near, far, turn=lambda block: block):
    a = place()[0]
    half, fourth = blocks // 2, blocks // 4

    def source(g):
        part, k = g % half // fourth, g % fourth
        cols = slice(k * QB, (k + 1) * QB)
        mine = jnp.where(a == part, own[:, cols], recv[:, cols]).astype(F32)
        theirs = jnp.where(near_part == part, near[:, cols], far[:, cols]).astype(F32)
        return jnp.where(mine_half == g // half, mine, turn(theirs))

    return source


def mid_step_body(own, recv, live, params, momentum, params_out, momentum_out, coded, scale,
                  *scratch):
    a = place()[0]
    blocks = params.shape[1] // QB
    half = blocks // 2

    def source(g):
        cols = slice(g % half * QB, (g % half + 1) * QB)
        return jnp.where(a == g // half, own[:, cols], recv[:, cols]).astype(F32)

    for copy in step_band(BAND, source, live, params, momentum, params_out, momentum_out, coded,
                          scale, *scratch):
        copy.wait()


def inner_step_body(own, recv, other, live, params, momentum, _p, _m, params_out, momentum_out,
                    coded, scale, *scratch):
    _, b, c = place()
    blocks = params.shape[1] // QB
    source = side_source(blocks, c, b, own, recv, other.at[0], other.at[1])
    for copy in step_band(side_rows(c)[0], source, live, params, momentum, params_out,
                          momentum_out, coded, scale, *scratch):
        copy.wait()


def outer_step_body(own, recv, other, coded_mid, scale_mid, coded_in, scale_in, live, params,
                    momentum, _p, _m, params_out, momentum_out, payload_out, scales_out, payload,
                    rows_scales, scales, *scratch):
    a, b, c = place()
    blocks = params.shape[1] // QB
    inner, outer = side_rows(c)
    payload[pl.ds(BAND, BAND), :] = coded_mid[...]
    payload[pl.ds(inner, BAND), :] = coded_in[...]
    rows_scales[pl.ds(BAND, BAND), :] = scale_mid[...]
    rows_scales[pl.ds(inner, BAND), :] = scale_in[...]
    source = side_source(blocks, 1 - c, jnp.where(at_end(), a, b), own, recv, other.at[0], other.at[1],
                         turned)
    copies = step_band(outer, source, live, params, momentum, params_out, momentum_out,
                       payload.at[pl.ds(outer, BAND)], rows_scales.at[pl.ds(outer, BAND)], *scratch)
    sems = scratch[-1]
    copies.append(pltpu.make_async_copy(payload, payload_out, sems.at[2, 0]))
    copies[-1].start()
    scales[...] = jnp.transpose(rows_scales[...])[:blocks, :]
    copies.append(pltpu.make_async_copy(scales, scales_out, sems.at[2, 1]))
    copies[-1].start()
    for copy in copies:
        copy.wait()


def shards(params, momentum, payload, scales, bounds):
    slots, width = payload.shape
    half, fourth, blocks = width // 2, width // 4, width // QB
    out_send, payload_near, rows_scales, live = local_call(
        outer_terms_body,
        [
            ((2, BAND, fourth), BF16, VMEM),
            ((slots, width), BF16, VMEM),
            ((slots, QB), F32, VMEM),
            ((slots, QB), F32, VMEM),
        ],
        [HBM, HBM, HBM],
        *(pltpu.with_memory_space_constraint(x, pltpu.HBM) for x in (payload, scales.T, bounds)),
        scratch=[
            pltpu.VMEM((blocks, slots), F32),
            pltpu.SMEM(bounds.shape, jnp.int32),
            pltpu.SemaphoreType.DMA((4,)),
        ],
    )
    out_recv = outer_swap(out_send)
    near = (payload_near, rows_scales)
    in_send, mid_send, mid_keep = local_call(
        mid_terms_body,
        [
            ((2, BAND, fourth), BF16, VMEM),
            ((BAND, half), BF16, VMEM),
            ((BAND, half), F32, VMEM),
        ],
        [VMEM] * 2,
        *near,
    )
    in_recv = inner_swap(in_send)
    in_first, in_keep, out_first, out_keep = local_call(
        side_terms_body,
        [((BAND, fourth), BF16, VMEM), ((BAND, fourth), F32, VMEM)] * 2,
        [VMEM] * 2,
        *near,
    )
    mid = add_to(island_swap(mid_send, 0), mid_keep)
    out_send, out_keep = add_to(out_first, out_recv[0]), add_to(out_keep, out_recv[1])
    out = add_to(island_swap(out_send, 0), out_keep)
    in_send, in_keep = add_to(in_first, in_recv[0]), add_to(in_keep, in_recv[1])
    inn = add_to(island_swap(in_send, 0), in_keep)
    mid = after(mid, in_send)
    own_mid = add_to(mid, island_swap(mid, 1))
    own_out = add_to(out, island_swap(out, 1))
    own_in = add_to(inn, island_swap(inn, 1))
    recv_mid = island_swap(own_mid, 0)
    own_in = after(own_in, own_mid)
    recv_out = island_swap(own_out, 0)
    out_other = outer_swap(jnp.stack([own_out, recv_out]))
    recv_in = island_swap(own_in, 0)
    in_other = inner_swap(jnp.stack([own_in, recv_in]))

    whole = ((slots, width), F32, HBM)
    band = [((BAND, width), BF16, VMEM), ((BAND, QB), F32, VMEM)]
    scratch = [
        pltpu.VMEM((BAND, width), F32),
        pltpu.VMEM((BAND, width), F32),
        pltpu.SemaphoreType.DMA((3, 4)),
    ]
    state = (live, params, momentum)
    params_out, momentum_out, coded_mid, scale_mid = local_call(
        mid_step_body, [whole, whole] + band, [VMEM] * 5, own_mid, recv_mid, *state,
        grant=4, scratch=scratch, cost=24,
    )
    params_out, momentum_out, coded_in, scale_in = local_call(
        inner_step_body, [whole, whole] + band, [VMEM] * 6 + [HBM] * 2, own_in, recv_in, in_other,
        *state, params_out, momentum_out,
        grant=4, scratch=scratch, cost=4, aliases={6: 0, 7: 1},
    )
    params_out, momentum_out, payload_out, scales_out = local_call(
        outer_step_body,
        [whole, whole, ((slots, width), BF16, HBM), ((blocks, slots), F32, HBM)],
        [VMEM] * 10 + [HBM] * 2,
        own_out, recv_out, out_other, coded_mid, scale_mid, coded_in, scale_in,
        *state, params_out, momentum_out,
        grant=6, cost=4, aliases={10: 0, 11: 1},
        scratch=[
            pltpu.VMEM((slots, width), BF16),
            pltpu.VMEM((slots, QB), F32),
            pltpu.VMEM((blocks, slots), F32),
        ] + scratch,
    )
    return params_out, momentum_out, payload_out, scales_out.T


def solution(mesh):
    spec = P(("island", "fsdp"), None)
    return jax.shard_map(
        shards, mesh=mesh, in_specs=(spec,) * 4 + (P(),), out_specs=(spec,) * 4, check_vma=False
    )
```

```python
import jax
import jax.numpy as jnp
from jax import lax
from jax.experimental import pallas as pl
from jax.experimental.pallas import tpu as pltpu
from jax.sharding import PartitionSpec as P

ROWS_DEV = 48
HALF = 12
BAND = 24
QB = 128

momentum_keep = 0.9
outer_rate = 0.7
block_eps = 1e-06

F32 = jnp.float32
BF16 = jnp.bfloat16
AXES = ("island", "fsdp")
PAIRINGS = ({0: 1, 1: 0, 2: 3, 3: 2}, {0: 3, 3: 0, 1: 2, 2: 1})


def island_swap(value, step):
    shards = lax.axis_size("fsdp")
    pairs = [
        (i * shards + j, PAIRINGS[(j + step) % 2][i] * shards + j)
        for i in range(4)
        for j in range(shards)
    ]
    return lax.ppermute(value, AXES, pairs)


def inner_swap(value):
    return lax.ppermute(value, "fsdp", [(j, j ^ 1) for j in range(lax.axis_size("fsdp"))])


def outer_swap(value):
    count = lax.axis_size("fsdp")
    pairs = []
    for i in range(4):
        for j in range(count):
            near = j + 1 if j & 1 else j - 1
            inside = 0 <= near < count
            pairs.append((i * count + j, i * count + near if inside else PAIRINGS[0][i] * count + j))
    return jnp.where(at_end(), value, lax.ppermute(value, AXES, pairs))


def place():
    island, odd = lax.axis_index("island"), lax.axis_index("fsdp") & 1
    low, high = island & 1, island >> 1
    return jnp.where(odd == 0, low ^ high, high), jnp.where(odd == 0, high, low ^ high), odd


VMEM = pl.BlockSpec(memory_space=pltpu.VMEM)
HBM = pl.BlockSpec(memory_space=pltpu.HBM)


def local_call(body, outs, ins, *arrays, grant=2, aliases=None, scratch=(), cost=1):
    return pl.pallas_call(
        body,
        out_shape=[jax.ShapeDtypeStruct(s, d) for s, d, _ in outs],
        in_specs=ins,
        out_specs=[space for _, _, space in outs],
        scratch_shapes=scratch,
        input_output_aliases=aliases or {},
        cost_estimate=pl.CostEstimate(
            flops=cost << 20, bytes_accessed=cost << 20, transcendentals=0
        ),
        compiler_params=pltpu.CompilerParams(vmem_limit_bytes=grant << 20),
    )(*arrays)


def at_end():
    shard = lax.axis_index("fsdp")
    return (shard == 0) | (shard == lax.axis_size("fsdp") - 1)


def turned(block):
    swapped = jnp.concatenate([block[HALF:], block[:HALF]])
    return jnp.where(at_end(), swapped, block)


def fill(payload, rows_scales, first, start, count, target, turn=lambda block: block):
    rows = pl.ds(first, BAND)
    local = pltpu.roll(rows_scales[rows, :], lax.rem(QB - start, QB), 1)
    for k in range(count):
        cols = pl.ds(pl.multiple_of((start + k) * QB, QB), QB)
        block = payload[rows, cols].astype(F32) * local[:, k : k + 1]
        target[:, k * QB : (k + 1) * QB] = turn(block).astype(target.dtype)


def side_rows(odd):
    return pl.multiple_of((1 - odd) * (2 * BAND), 16), pl.multiple_of(odd * (2 * BAND), 16)


def outer_terms_body(payload_in, scales_in, bounds_in, out_send, payload, rows_scales, live, scales,
                     bounds, sems):
    a, b, c = place()
    slots, width = payload.shape
    blocks = width // QB
    half, fourth = blocks // 2, blocks // 4
    copies = [pltpu.make_async_copy(bounds_in, bounds, sems.at[0])]
    copies.append(pltpu.make_async_copy(scales_in, scales, sems.at[1]))
    for n, part in enumerate((c, 1 - c)):
        cols = pl.ds(pl.multiple_of(part * (width // 2), QB), width // 2)
        copies.append(
            pltpu.make_async_copy(payload_in.at[:, cols], payload.at[:, cols], sems.at[2 + n])
        )
    for copy in copies:
        copy.start()
    copies[0].wait()
    island, shard = lax.axis_index("island"), lax.axis_index("fsdp")
    origin = shard * ROWS_DEV - HALF
    row = lax.broadcasted_iota(jnp.int32, (slots, QB), 0) + origin
    live[...] = ((row >= bounds[island, shard]) & (row < bounds[island, shard + 1])).astype(F32)
    rows_scales[...] = jnp.zeros(rows_scales.shape, F32)
    copies[1].wait()
    rows_scales[:, :blocks] = jnp.transpose(scales[...]) * live[:, :blocks]
    outer = side_rows(c)[1]
    copies[2].wait()
    for u in range(2):
        part = (jnp.where(at_end(), a, b) ^ 1 ^ u) * fourth
        fill(payload, rows_scales, outer, c * half + part, fourth, out_send.at[u], turned)
    copies[3].wait()


def mid_terms_body(payload, rows_scales, in_send, send, keep):
    a, b, c = place()
    blocks = payload.shape[1] // QB
    half, fourth = blocks // 2, blocks // 4
    for u in range(2):
        start = (1 - c) * half + (b ^ 1 ^ u) * fourth
        fill(payload, rows_scales, side_rows(c)[0], start, fourth, in_send.at[u])
    fill(payload, rows_scales, BAND, (1 - a) * half, half, send)
    fill(payload, rows_scales, BAND, a * half, half, keep)


def side_terms_body(payload, rows_scales, in_first, in_keep, out_first, out_keep):
    a, _, c = place()
    blocks = payload.shape[1] // QB
    half, fourth = blocks // 2, blocks // 4
    inner, outer = side_rows(c)
    for part, near, far in ((1 - a, in_first, out_first), (a, in_keep, out_keep)):
        fill(payload, rows_scales, inner, c * half + part * fourth, fourth, near)
        fill(payload, rows_scales, outer, (1 - c) * half + part * fourth, fourth, far)


def add_to(total, part):
    return (total.astype(F32) + part.astype(F32)).astype(total.dtype)


def after(value, *others):
    return lax.optimization_barrier((value, others))[0]


def step_band(first, source, live, params, momentum, params_out, momentum_out, coded_out,
              scale_out, params_new, momentum_new, sems):
    rows = pl.ds(first, BAND)
    blocks = params.shape[1] // QB
    fourth = blocks // 4
    lane = lax.broadcasted_iota(jnp.int32, (BAND, QB), 1)
    alive = live[rows, :]
    scale_row = jnp.zeros((BAND, QB), F32)
    copies = []
    for g in range(blocks):
        cols = slice(g * QB, (g + 1) * QB)
        summed = source(g)
        block_scale = jnp.max(jnp.abs(summed), axis=1, keepdims=True) + block_eps
        coded = (summed * (1.0 / block_scale)).astype(BF16).astype(F32) * alive
        block_live = block_scale * alive
        delta = coded * (block_live * 0.25)
        moved = momentum_keep * momentum[rows, cols] + delta
        momentum_new[:, cols] = moved
        params_new[:, cols] = params[rows, cols] - outer_rate * (delta + momentum_keep * moved)
        coded_out[:, cols] = coded.astype(BF16)
        scale_row = jnp.where(lane == g, block_live, scale_row)
        if g % fourth == fourth - 1:
            part = slice((g + 1 - fourth) * QB, (g + 1) * QB)
            for n, (new, out) in enumerate(
                ((params_new, params_out), (momentum_new, momentum_out))
            ):
                copy = pltpu.make_async_copy(
                    new.at[:, part], out.at[rows, part], sems.at[n, g // fourth]
                )
                copy.start()
                copies.append(copy)
    scale_out[...] = scale_row
    return copies


def side_source(blocks, mine_half, near_part, own, recv, near, far, turn=lambda block: block):
    a = place()[0]
    half, fourth = blocks // 2, blocks // 4

    def source(g):
        part, k = g % half // fourth, g % fourth
        cols = slice(k * QB, (k + 1) * QB)
        mine = jnp.where(a == part, own[:, cols], recv[:, cols]).astype(F32)
        theirs = jnp.where(near_part == part, near[:, cols], far[:, cols]).astype(F32)
        return jnp.where(mine_half == g // half, mine, turn(theirs))

    return source


def mid_step_body(own, recv, live, params, momentum, params_out, momentum_out, coded, scale,
                  *scratch):
    a = place()[0]
    blocks = params.shape[1] // QB
    half = blocks // 2

    def source(g):
        cols = slice(g % half * QB, (g % half + 1) * QB)
        return jnp.where(a == g // half, own[:, cols], recv[:, cols]).astype(F32)

    for copy in step_band(BAND, source, live, params, momentum, params_out, momentum_out, coded,
                          scale, *scratch):
        copy.wait()


def outer_step_body(own, recv, other, live, params, momentum, _p, _m, params_out, momentum_out,
                    coded, scale, *scratch):
    a, b, c = place()
    source = side_source(params.shape[1] // QB, 1 - c, jnp.where(at_end(), a, b), own, recv,
                         other.at[0], other.at[1], turned)
    for copy in step_band(side_rows(c)[1], source, live, params, momentum, params_out,
                          momentum_out, coded, scale, *scratch):
        copy.wait()


def inner_step_body(own, recv, other, coded_mid, scale_mid, coded_out, scale_out, live, params,
                    momentum, _p, _m, params_out, momentum_out, payload_out, scales_out, payload,
                    rows_scales, scales, *scratch):
    _, b, c = place()
    blocks = params.shape[1] // QB
    inner, outer = side_rows(c)
    payload[pl.ds(BAND, BAND), :] = coded_mid[...]
    payload[pl.ds(outer, BAND), :] = coded_out[...]
    rows_scales[pl.ds(BAND, BAND), :] = scale_mid[...]
    rows_scales[pl.ds(outer, BAND), :] = scale_out[...]
    source = side_source(blocks, c, b, own, recv, other.at[0], other.at[1])
    copies = step_band(inner, source, live, params, momentum, params_out, momentum_out,
                       payload.at[pl.ds(inner, BAND)], rows_scales.at[pl.ds(inner, BAND)], *scratch)
    sems = scratch[-1]
    copies.append(pltpu.make_async_copy(payload, payload_out, sems.at[2, 0]))
    copies[-1].start()
    scales[...] = jnp.transpose(rows_scales[...])[:blocks, :]
    copies.append(pltpu.make_async_copy(scales, scales_out, sems.at[2, 1]))
    copies[-1].start()
    for copy in copies:
        copy.wait()


def shards(params, momentum, payload, scales, bounds):
    slots, width = payload.shape
    half, fourth, blocks = width // 2, width // 4, width // QB
    out_send, payload_near, rows_scales, live = local_call(
        outer_terms_body,
        [
            ((2, BAND, fourth), BF16, VMEM),
            ((slots, width), BF16, VMEM),
            ((slots, QB), F32, VMEM),
            ((slots, QB), F32, VMEM),
        ],
        [HBM, HBM, HBM],
        *(pltpu.with_memory_space_constraint(x, pltpu.HBM) for x in (payload, scales.T, bounds)),
        scratch=[
            pltpu.VMEM((blocks, slots), F32),
            pltpu.SMEM(bounds.shape, jnp.int32),
            pltpu.SemaphoreType.DMA((4,)),
        ],
    )
    out_recv = outer_swap(out_send)
    near = (payload_near, rows_scales)
    in_send, mid_send, mid_keep = local_call(
        mid_terms_body,
        [
            ((2, BAND, fourth), BF16, VMEM),
            ((BAND, half), BF16, VMEM),
            ((BAND, half), F32, VMEM),
        ],
        [VMEM] * 2,
        *near,
    )
    in_recv = inner_swap(in_send)
    in_first, in_keep, out_first, out_keep = local_call(
        side_terms_body,
        [((BAND, fourth), BF16, VMEM), ((BAND, fourth), F32, VMEM)] * 2,
        [VMEM] * 2,
        *near,
    )
    mid = add_to(island_swap(mid_send, 0), mid_keep)
    out_send, out_keep = add_to(out_first, out_recv[0]), add_to(out_keep, out_recv[1])
    out = add_to(island_swap(out_send, 0), out_keep)
    in_send, in_keep = add_to(in_first, in_recv[0]), add_to(in_keep, in_recv[1])
    inn = add_to(island_swap(in_send, 0), in_keep)
    mid = after(mid, in_send)
    own_mid = add_to(mid, island_swap(mid, 1))
    own_out = add_to(out, island_swap(out, 1))
    own_in = add_to(inn, island_swap(inn, 1))
    recv_mid = island_swap(own_mid, 0)
    own_in = after(own_in, own_mid)
    recv_out = island_swap(own_out, 0)
    out_other = outer_swap(jnp.stack([own_out, recv_out]))
    recv_in = island_swap(own_in, 0)
    in_other = inner_swap(jnp.stack([own_in, recv_in]))

    whole = ((slots, width), F32, HBM)
    band = [((BAND, width), BF16, VMEM), ((BAND, QB), F32, VMEM)]
    scratch = [
        pltpu.VMEM((BAND, width), F32),
        pltpu.VMEM((BAND, width), F32),
        pltpu.SemaphoreType.DMA((3, 4)),
    ]
    state = (live, params, momentum)
    params_out, momentum_out, coded_mid, scale_mid = local_call(
        mid_step_body, [whole, whole] + band, [VMEM] * 5, own_mid, recv_mid, *state,
        grant=4, scratch=scratch, cost=24,
    )
    params_out, momentum_out, coded_out, scale_out = local_call(
        outer_step_body, [whole, whole] + band, [VMEM] * 6 + [HBM] * 2, own_out, recv_out, out_other,
        *state, params_out, momentum_out,
        grant=4, scratch=scratch, cost=4, aliases={6: 0, 7: 1},
    )
    params_out, momentum_out, payload_out, scales_out = local_call(
        inner_step_body,
        [whole, whole, ((slots, width), BF16, HBM), ((blocks, slots), F32, HBM)],
        [VMEM] * 10 + [HBM] * 2,
        own_in, recv_in, in_other, coded_mid, scale_mid, coded_out, scale_out,
        *state, params_out, momentum_out,
        grant=6, cost=4, aliases={10: 0, 11: 1},
        scratch=[
            pltpu.VMEM((slots, width), BF16),
            pltpu.VMEM((slots, QB), F32),
            pltpu.VMEM((blocks, slots), F32),
        ] + scratch,
    )
    return params_out, momentum_out, payload_out, scales_out.T


def solution(mesh):
    spec = P(("island", "fsdp"), None)
    return jax.shard_map(
        shards, mesh=mesh, in_specs=(spec,) * 4 + (P(),), out_specs=(spec,) * 4, check_vma=False
    )
```

```python
import jax
import jax.numpy as jnp
from jax import lax
from jax.experimental import pallas as pl
from jax.experimental.pallas import tpu as pltpu
from jax.sharding import PartitionSpec as P

ROWS_DEV = 48
HALF = 12
BAND = 24
QB = 128

momentum_keep = 0.9
outer_rate = 0.7
block_eps = 1e-06

F32 = jnp.float32
BF16 = jnp.bfloat16
AXES = ("island", "fsdp")
PAIRINGS = ({0: 1, 1: 0, 2: 3, 3: 2}, {0: 3, 3: 0, 1: 2, 2: 1})


def island_swap(value, step):
    shards = lax.axis_size("fsdp")
    pairs = [
        (i * shards + j, PAIRINGS[(j + step) % 2][i] * shards + j)
        for i in range(4)
        for j in range(shards)
    ]
    return lax.ppermute(value, AXES, pairs)


def inner_swap(value):
    return lax.ppermute(value, "fsdp", [(j, j ^ 1) for j in range(lax.axis_size("fsdp"))])


def outer_swap(value):
    count = lax.axis_size("fsdp")
    pairs = []
    for i in range(4):
        for j in range(count):
            near = j + 1 if j & 1 else j - 1
            inside = 0 <= near < count
            pairs.append((i * count + j, i * count + near if inside else PAIRINGS[0][i] * count + j))
    return jnp.where(at_end(), value, lax.ppermute(value, AXES, pairs))


def place():
    island, odd = lax.axis_index("island"), lax.axis_index("fsdp") & 1
    low, high = island & 1, island >> 1
    return jnp.where(odd == 0, low ^ high, high), jnp.where(odd == 0, high, low ^ high), odd


VMEM = pl.BlockSpec(memory_space=pltpu.VMEM)
HBM = pl.BlockSpec(memory_space=pltpu.HBM)


def local_call(body, outs, ins, *arrays, grant=2, aliases=None, scratch=(), cost=1):
    return pl.pallas_call(
        body,
        out_shape=[jax.ShapeDtypeStruct(s, d) for s, d, _ in outs],
        in_specs=ins,
        out_specs=[space for _, _, space in outs],
        scratch_shapes=scratch,
        input_output_aliases=aliases or {},
        cost_estimate=pl.CostEstimate(
            flops=cost << 20, bytes_accessed=cost << 20, transcendentals=0
        ),
        compiler_params=pltpu.CompilerParams(vmem_limit_bytes=grant << 20),
    )(*arrays)


def at_end():
    shard = lax.axis_index("fsdp")
    return (shard == 0) | (shard == lax.axis_size("fsdp") - 1)


def turned(block):
    swapped = jnp.concatenate([block[HALF:], block[:HALF]])
    return jnp.where(at_end(), swapped, block)


def fill(payload, rows_scales, first, start, count, target, turn=lambda block: block):
    rows = pl.ds(first, BAND)
    local = pltpu.roll(rows_scales[rows, :], lax.rem(QB - start, QB), 1)
    for k in range(count):
        cols = pl.ds(pl.multiple_of((start + k) * QB, QB), QB)
        block = payload[rows, cols].astype(F32) * local[:, k : k + 1]
        target[:, k * QB : (k + 1) * QB] = turn(block).astype(target.dtype)


def side_rows(odd):
    return pl.multiple_of((1 - odd) * (2 * BAND), 16), pl.multiple_of(odd * (2 * BAND), 16)


def outer_terms_body(payload_in, scales_in, bounds_in, out_send, payload, rows_scales, live, scales,
                     bounds, sems):
    a, b, c = place()
    slots, width = payload.shape
    blocks = width // QB
    half, fourth = blocks // 2, blocks // 4
    copies = [pltpu.make_async_copy(bounds_in, bounds, sems.at[0])]
    copies.append(pltpu.make_async_copy(scales_in, scales, sems.at[1]))
    for n, part in enumerate((c, 1 - c)):
        cols = pl.ds(pl.multiple_of(part * (width // 2), QB), width // 2)
        copies.append(
            pltpu.make_async_copy(payload_in.at[:, cols], payload.at[:, cols], sems.at[2 + n])
        )
    for copy in copies:
        copy.start()
    copies[0].wait()
    island, shard = lax.axis_index("island"), lax.axis_index("fsdp")
    origin = shard * ROWS_DEV - HALF
    row = lax.broadcasted_iota(jnp.int32, (slots, QB), 0) + origin
    live[...] = ((row >= bounds[island, shard]) & (row < bounds[island, shard + 1])).astype(F32)
    rows_scales[...] = jnp.zeros(rows_scales.shape, F32)
    copies[1].wait()
    rows_scales[:, :blocks] = jnp.transpose(scales[...]) * live[:, :blocks]
    outer = side_rows(c)[1]
    copies[2].wait()
    for u in range(2):
        part = (jnp.where(at_end(), a, b) ^ 1 ^ u) * fourth
        fill(payload, rows_scales, outer, c * half + part, fourth, out_send.at[u], turned)
    copies[3].wait()


def mid_terms_body(payload, rows_scales, in_send, send, keep):
    a, b, c = place()
    blocks = payload.shape[1] // QB
    half, fourth = blocks // 2, blocks // 4
    for u in range(2):
        start = (1 - c) * half + (b ^ 1 ^ u) * fourth
        fill(payload, rows_scales, side_rows(c)[0], start, fourth, in_send.at[u])
    fill(payload, rows_scales, BAND, (1 - a) * half, half, send)
    fill(payload, rows_scales, BAND, a * half, half, keep)


def side_terms_body(payload, rows_scales, in_first, in_keep, out_first, out_keep):
    a, _, c = place()
    blocks = payload.shape[1] // QB
    half, fourth = blocks // 2, blocks // 4
    inner, outer = side_rows(c)
    for part, near, far in ((1 - a, in_first, out_first), (a, in_keep, out_keep)):
        fill(payload, rows_scales, inner, c * half + part * fourth, fourth, near)
        fill(payload, rows_scales, outer, (1 - c) * half + part * fourth, fourth, far)


def add_to(total, part):
    return (total.astype(F32) + part.astype(F32)).astype(total.dtype)


def after(value, *others):
    return lax.optimization_barrier((value, others))[0]


def step_band(first, source, live, params, momentum, params_out, momentum_out, coded_out,
              scale_out, params_new, momentum_new, sems, all_rows=()):
    rows = pl.ds(first, BAND)
    blocks = params.shape[1] // QB
    fourth = blocks // 4
    lane = lax.broadcasted_iota(jnp.int32, (BAND, QB), 1)
    alive = live[rows, :]
    scale_row = jnp.zeros((BAND, QB), F32)
    copies = []
    for g in range(blocks):
        cols = slice(g * QB, (g + 1) * QB)
        summed = source(g)
        block_scale = jnp.max(jnp.abs(summed), axis=1, keepdims=True) + block_eps
        coded = (summed * (1.0 / block_scale)).astype(BF16).astype(F32) * alive
        block_live = block_scale * alive
        delta = coded * (block_live * 0.25)
        moved = momentum_keep * momentum[rows, cols] + delta
        momentum_new[:, cols] = moved
        params_new[:, cols] = params[rows, cols] - outer_rate * (delta + momentum_keep * moved)
        coded_out[:, cols] = coded.astype(BF16)
        scale_row = jnp.where(lane == g, block_live, scale_row)
        if g % fourth == fourth - 1:
            part = slice((g + 1 - fourth) * QB, (g + 1) * QB)
            for n, (new, out) in enumerate(
                ((params_new, params_out), (momentum_new, momentum_out))
            ):
                copy = pltpu.make_async_copy(
                    new.at[:, part], out.at[rows, part], sems.at[n, g // fourth]
                )
                copy.start()
                copies.append(copy)
            for new, out in all_rows:
                copy = pltpu.make_async_copy(
                    new.at[:, part], out.at[:, part], sems.at[2, g // fourth]
                )
                copy.start()
                copies.append(copy)
    scale_out[...] = scale_row
    return copies


def side_source(blocks, mine_half, near_part, own, recv, near, far, turn=lambda block: block):
    a = place()[0]
    half, fourth = blocks // 2, blocks // 4

    def source(g):
        part, k = g % half // fourth, g % fourth
        cols = slice(k * QB, (k + 1) * QB)
        mine = jnp.where(a == part, own[:, cols], recv[:, cols]).astype(F32)
        theirs = jnp.where(near_part == part, near[:, cols], far[:, cols]).astype(F32)
        return jnp.where(mine_half == g // half, mine, turn(theirs))

    return source


def mid_step_body(own, recv, live, params, momentum, params_out, momentum_out, coded, scale,
                  *scratch):
    a = place()[0]
    blocks = params.shape[1] // QB
    half = blocks // 2

    def source(g):
        cols = slice(g % half * QB, (g % half + 1) * QB)
        return jnp.where(a == g // half, own[:, cols], recv[:, cols]).astype(F32)

    for copy in step_band(BAND, source, live, params, momentum, params_out, momentum_out, coded,
                          scale, *scratch):
        copy.wait()


def outer_step_body(own, recv, other, live, params, momentum, _p, _m, params_out, momentum_out,
                    coded, scale, *scratch):
    a, b, c = place()
    source = side_source(params.shape[1] // QB, 1 - c, jnp.where(at_end(), a, b), own, recv,
                         other.at[0], other.at[1], turned)
    for copy in step_band(side_rows(c)[1], source, live, params, momentum, params_out,
                          momentum_out, coded, scale, *scratch):
        copy.wait()


def inner_step_body(own, recv, other, coded_mid, scale_mid, coded_out, scale_out, live, params,
                    momentum, _p, _m, params_out, momentum_out, payload_out, scales_out, payload,
                    rows_scales, scales, *scratch):
    _, b, c = place()
    blocks = params.shape[1] // QB
    inner, outer = side_rows(c)
    payload[pl.ds(BAND, BAND), :] = coded_mid[...]
    payload[pl.ds(outer, BAND), :] = coded_out[...]
    rows_scales[pl.ds(BAND, BAND), :] = scale_mid[...]
    rows_scales[pl.ds(outer, BAND), :] = scale_out[...]
    source = side_source(blocks, c, b, own, recv, other.at[0], other.at[1])
    copies = step_band(inner, source, live, params, momentum, params_out, momentum_out,
                       payload.at[pl.ds(inner, BAND)], rows_scales.at[pl.ds(inner, BAND)], *scratch,
                       all_rows=[(payload, payload_out)])
    sems = scratch[-1]
    scales[...] = jnp.transpose(rows_scales[...])[:blocks, :]
    copies.append(pltpu.make_async_copy(scales, scales_out, sems.at[3, 0]))
    copies[-1].start()
    for copy in copies:
        copy.wait()


def shards(params, momentum, payload, scales, bounds):
    slots, width = payload.shape
    half, fourth, blocks = width // 2, width // 4, width // QB
    out_send, payload_near, rows_scales, live = local_call(
        outer_terms_body,
        [
            ((2, BAND, fourth), BF16, VMEM),
            ((slots, width), BF16, VMEM),
            ((slots, QB), F32, VMEM),
            ((slots, QB), F32, VMEM),
        ],
        [HBM, HBM, HBM],
        *(pltpu.with_memory_space_constraint(x, pltpu.HBM) for x in (payload, scales.T, bounds)),
        scratch=[
            pltpu.VMEM((blocks, slots), F32),
            pltpu.SMEM(bounds.shape, jnp.int32),
            pltpu.SemaphoreType.DMA((4,)),
        ],
    )
    out_recv = outer_swap(out_send)
    near = (payload_near, rows_scales)
    in_send, mid_send, mid_keep = local_call(
        mid_terms_body,
        [
            ((2, BAND, fourth), BF16, VMEM),
            ((BAND, half), BF16, VMEM),
            ((BAND, half), F32, VMEM),
        ],
        [VMEM] * 2,
        *near,
    )
    in_recv = inner_swap(in_send)
    in_first, in_keep, out_first, out_keep = local_call(
        side_terms_body,
        [((BAND, fourth), BF16, VMEM), ((BAND, fourth), F32, VMEM)] * 2,
        [VMEM] * 2,
        *near,
    )
    mid = add_to(island_swap(mid_send, 0), mid_keep)
    out_send, out_keep = add_to(out_first, out_recv[0]), add_to(out_keep, out_recv[1])
    out = add_to(island_swap(out_send, 0), out_keep)
    in_send, in_keep = add_to(in_first, in_recv[0]), add_to(in_keep, in_recv[1])
    inn = add_to(island_swap(in_send, 0), in_keep)
    mid = after(mid, in_send)
    own_mid = add_to(mid, island_swap(mid, 1))
    own_out = add_to(out, island_swap(out, 1))
    own_in = add_to(inn, island_swap(inn, 1))
    recv_mid = island_swap(own_mid, 0)
    own_in = after(own_in, own_mid)
    recv_out = island_swap(own_out, 0)
    out_other = outer_swap(jnp.stack([own_out, recv_out]))
    recv_in = island_swap(own_in, 0)
    in_other = inner_swap(jnp.stack([own_in, recv_in]))

    whole = ((slots, width), F32, HBM)
    band = [((BAND, width), BF16, VMEM), ((BAND, QB), F32, VMEM)]
    scratch = [
        pltpu.VMEM((BAND, width), F32),
        pltpu.VMEM((BAND, width), F32),
        pltpu.SemaphoreType.DMA((4, 4)),
    ]
    state = (live, params, momentum)
    params_out, momentum_out, coded_mid, scale_mid = local_call(
        mid_step_body, [whole, whole] + band, [VMEM] * 5, own_mid, recv_mid, *state,
        grant=4, scratch=scratch, cost=24,
    )
    params_out, momentum_out, coded_out, scale_out = local_call(
        outer_step_body, [whole, whole] + band, [VMEM] * 6 + [HBM] * 2, own_out, recv_out, out_other,
        *state, params_out, momentum_out,
        grant=4, scratch=scratch, cost=4, aliases={6: 0, 7: 1},
    )
    params_out, momentum_out, payload_out, scales_out = local_call(
        inner_step_body,
        [whole, whole, ((slots, width), BF16, HBM), ((blocks, slots), F32, HBM)],
        [VMEM] * 10 + [HBM] * 2,
        own_in, recv_in, in_other, coded_mid, scale_mid, coded_out, scale_out,
        *state, params_out, momentum_out,
        grant=6, cost=4, aliases={10: 0, 11: 1},
        scratch=[
            pltpu.VMEM((slots, width), BF16),
            pltpu.VMEM((slots, QB), F32),
            pltpu.VMEM((blocks, slots), F32),
        ] + scratch,
    )
    return params_out, momentum_out, payload_out, scales_out.T


def solution(mesh):
    spec = P(("island", "fsdp"), None)
    return jax.shard_map(
        shards, mesh=mesh, in_specs=(spec,) * 4 + (P(),), out_specs=(spec,) * 4, check_vma=False
    )
```
